256 devices in a mesh: ctx: 32 (over z, x_lo, core), head: 8 (over y, x_hi).
Axes of the slice: x: 4 (x_hi: 2, x_lo: 2; x = x_hi * 2 + x_lo), y: 4, z: 8, core: 2. Of those that a mesh axis runs over, the one named last changes fastest.
Arguments:
- q_latent: bfloat16 [4096, 1536], P('ctx'), may hold values from -6 to 6
- kv_latent: bfloat16 [4096, 576], P('ctx'), may hold values from -420 to 420
- q_gain: float32 [1536], replicated, may hold values from 0.1 to 1.9
- kv_gain: float32 [512], replicated, may hold values from 0.1 to 1.9
- q_up: bfloat16 [1536, 12288], P(None, 'head'), may hold values from -0.15625 to 0.15625
- kv_up: bfloat16 [512, 16384], P(None, 'head'), may hold values from -0.25 to 0.25
- out_proj: bfloat16 [8192, 7168], P(('head', 'ctx')), may hold values from -0.5 to 0.5
- segment_ids: int32 [4096], replicated, may hold values from 0 to 7, never falling along the last dimension, each value on 1 to 1024 neighbouring positions
- trace_limit: int32 [8], replicated, may hold values from 1 to 1024
Outputs:
- mixed: bfloat16 [4096, 7168], P('ctx', 'head')
The draws below stay inside these ranges and needn't reach their ends.
Inputs may be any that keep to these rules, and one draw needn't show every extreme that they name: `segment_ids`: trace numbers never fall along the window; each trace holds 1 to 1024 tokens, one exactly 1024.
All inputs are finite; a program needn't handle non-finite values.
Results may differ from the reference program's by a relative error of at most 0.025.
The reference program's roundings to bfloat16 on the way count: a program that leaves them out, or rounds other values in their place, can miss the bound.
Values may be sent and summed in bfloat16 or wider, within the bound.
A program may use at most 128 MiB of HBM per device.

```python
import math
import jax
import jax.numpy as jnp
import numpy as np
from jax import lax

D = 7168
HEADS = 64
Q_RANK = 1536
KV_RANK = 512
QK_NOPE = 128
QK_ROPE = 64
V_DIM = 128
TOKENS = 4096
TRACES = 8
MOST = 1024


def draw_kv_latent(key, part):
    key = jax.random.fold_in(key, 7)
    first_key = jax.random.fold_in(key, 0)
    columns = KV_RANK + QK_ROPE
    return jnp.clip(jax.random.normal(first_key, (TOKENS, columns), jnp.float32), -6.0, 6.0).astype(jnp.bfloat16)


def touch_ends(values, stream_key, smallest, top_value):
    extent = values.shape
    spot = [jax.random.randint(jax.random.fold_in(stream_key, axis), (), 0, extent[axis]) for axis in range(len(extent))]
    values = values.at[tuple(spot)].set(smallest)
    longest = extent.index(max(extent))
    spot[longest] = (spot[longest] + 1) % extent[longest]
    return values.at[tuple(spot)].set(top_value)


def levels(key, shape, pieces, least, high):
    level, own = 1.0, jax.random.fold_in(key, 6)
    for position, parts in pieces:
        steps = jnp.exp(jax.random.uniform(jax.random.fold_in(own, position), (parts,), jnp.float32, least / len(pieces), high / len(pieces)))
        level = level * jnp.repeat(steps, shape[position] // parts).reshape([-1 if axis == position else 1 for axis in range(len(shape))])
    return level


def split_up(count, total, most, slope):
    portions = [(1 << 20) // math.isqrt(grade ** slope) + 1 for grade in range(2, count + 1)]
    rest, counts = total - most - (count - 1), [1] * (count - 1)
    while rest > 0:
        candidates = [i for i in range(count - 1) if counts[i] < most]
        whole, budget = sum([portions[i] for i in candidates]), rest
        for i in candidates:
            extra = min(most - counts[i], max(1, budget * portions[i] // whole), rest)
            counts[i] = counts[i] + extra
            rest = rest - extra
    return np.array([most] + counts)


def uneven_parts(own_key, number_of, total, most, lean):
    if number_of == 2:
        one = jax.random.randint(own_key, (), max(1, total - most), min(most, total - 1) + 1)
        return jnp.stack([one, total - one])
    tallies = jnp.asarray(split_up(number_of, total, most, lean), jnp.int32)
    couples = (number_of - 1) // 2
    giver, taker = tallies[1:1 + 2 * couples:2], tallies[2:2 + 2 * couples:2]
    margin = jnp.minimum(giver - 1, most - taker)
    passed = jax.random.randint(jax.random.fold_in(own_key, 1), (couples,), 0, 1 << 20) % (margin + 1)
    tallies = tallies.at[1:1 + 2 * couples:2].set(giver - passed).at[2:2 + 2 * couples:2].set(taker + passed)
    return tallies[jax.random.permutation(jax.random.fold_in(own_key, 2), number_of)]


def noise(key, dims, deviation, limit, shards=(), held_as=jnp.bfloat16):
    values = deviation * jax.random.normal(key, dims, jnp.float32)
    if shards:
        values = values * levels(key, dims, shards, -0.22, 0.18)
    return jnp.clip(values, -limit, limit).astype(held_as)


def setup_inputs(seed: int = 0) -> dict:
    arg_keys = jax.random.split(jax.random.key(seed), 10)
    q_latent = noise(arg_keys[0], (TOKENS, Q_RANK), 1.0, 6.0, ((0, 32),))
    kv_latent = draw_kv_latent(jax.random.fold_in(arg_keys[9], 71), 0)
    q_gain = jnp.clip(1.0 + 0.18 * jax.random.normal(arg_keys[2], (Q_RANK,), jnp.float32), 0.1, 1.9)
    kv_gain = jnp.clip(1.0 + 0.18 * jax.random.normal(arg_keys[3], (KV_RANK,), jnp.float32), 0.1, 1.9)
    q_up = noise(arg_keys[4], (Q_RANK, HEADS * (QK_NOPE + QK_ROPE)), Q_RANK ** -0.5, 0.15625, ((1, 8),))
    kv_up = noise(arg_keys[5], (KV_RANK, HEADS * (QK_NOPE + V_DIM)), KV_RANK ** -0.5, 0.25, ((1, 8),))
    out_proj = noise(arg_keys[6], (HEADS * V_DIM, D), V_DIM ** -0.5, 0.5, ((0, 256),))
    segment_ids = jnp.searchsorted(jnp.cumsum(uneven_parts(arg_keys[7], TRACES, TOKENS, MOST, 2)), jnp.arange(TOKENS), side="right").astype(jnp.int32)
    trace_limit = touch_ends(jax.random.randint(arg_keys[8], (TRACES,), 1, MOST + 1), jax.random.fold_in(arg_keys[8], 1), 1, MOST).astype(jnp.int32)
    return {"q_latent": q_latent, "kv_latent": kv_latent, "q_gain": q_gain, "kv_gain": kv_gain, "q_up": q_up, "kv_up": kv_up, "out_proj": out_proj, "segment_ids": segment_ids, "trace_limit": trace_limit}


def rms_scale(values, gain):
    return values * lax.rsqrt(lax.optimization_barrier(jnp.mean(values * values, axis=-1, keepdims=True)) + 1e-06) * gain

def rotate(values, places):
    half = values.shape[-1] // 2
    inverse = 10000.0 ** (-jnp.arange(half, dtype=jnp.float32) / half)
    angles = places.astype(jnp.float32)[:, None] * inverse[None, :]
    cosine = jnp.cos(angles)
    sine = jnp.sin(angles)
    if values.ndim == 3:
        cosine = cosine[:, None, :]
        sine = sine[:, None, :]
    first = values[..., :half]
    second = values[..., half:]
    return jnp.concatenate([first * cosine - second * sine, first * sine + second * cosine], axis=-1)

def token_flags(segment_ids, trace_limit):
    traces = trace_limit.shape[0]
    count = segment_ids.shape[0]
    numbers = jnp.arange(traces, dtype=jnp.int32)
    onehot = (segment_ids[:, None] == numbers[None, :]).astype(jnp.int32)
    before = (segment_ids[:, None] < numbers[None, :]).astype(jnp.int32)
    starts = lax.optimization_barrier(jnp.sum(before, axis=0))
    start_tok = lax.optimization_barrier(jnp.sum(onehot * starts[None, :], axis=1))
    limit_tok = lax.optimization_barrier(jnp.sum(onehot * trace_limit[None, :], axis=1))
    place = jnp.arange(count, dtype=jnp.int32) - start_tok
    return place < limit_tok

def reference(q_latent, kv_latent, q_gain, kv_gain, q_up, kv_up, out_proj, segment_ids, trace_limit):
    tokens = q_latent.shape[0]
    places = jnp.arange(tokens, dtype=jnp.int32)
    qnorm = rms_scale(q_latent.astype(jnp.float32), q_gain).astype(jnp.bfloat16)
    qfull = jnp.dot(qnorm, q_up, preferred_element_type=jnp.float32).reshape(tokens, HEADS, QK_NOPE + QK_ROPE)
    query = jnp.concatenate([qfull[..., :QK_NOPE], rotate(qfull[..., QK_NOPE:], places)], axis=-1).astype(jnp.bfloat16)
    latent = jnp.concatenate([rms_scale(kv_latent[:, :KV_RANK].astype(jnp.float32), kv_gain), rotate(kv_latent[:, KV_RANK:].astype(jnp.float32), places)], axis=-1).astype(jnp.bfloat16)
    keyval = jnp.dot(latent[:, :KV_RANK], kv_up, preferred_element_type=jnp.float32).astype(jnp.bfloat16)
    keyval = lax.optimization_barrier(keyval).astype(jnp.float32).reshape(tokens, HEADS, QK_NOPE + V_DIM)
    key_nope = keyval[..., :QK_NOPE]
    value = keyval[..., QK_NOPE:]
    key_rope = latent[:, KV_RANK:].astype(jnp.float32)
    kept = token_flags(segment_ids, trace_limit)
    scale = (QK_NOPE + QK_ROPE) ** (-0.5)
    block = min(256, tokens)
    count = tokens // block

    def one_block(index):
        first = (index * block).astype(jnp.int32)
        queries = lax.dynamic_slice_in_dim(query, first, block, 0).astype(jnp.float32)
        qplace = first + jnp.arange(block, dtype=jnp.int32)
        qseg = lax.dynamic_slice_in_dim(segment_ids, first, block, 0)
        visible = (qseg[:, None] == segment_ids[None, :]) & (places[None, :] <= qplace[:, None]) & kept[None, :]
        scores = jnp.einsum('thd,khd->htk', queries[..., :QK_NOPE], key_nope)
        scores = (scores + jnp.einsum('thd,kd->htk', queries[..., QK_NOPE:], key_rope)) * scale
        masked = jnp.where(visible[None], scores, -1e+30)
        top = lax.optimization_barrier(jnp.max(masked, axis=-1, keepdims=True))
        weights = jnp.where(visible[None], jnp.exp(masked - top), 0.0)
        total = lax.optimization_barrier(jnp.sum(weights, axis=-1))
        rounded = lax.optimization_barrier(weights.astype(jnp.bfloat16)).astype(jnp.float32)
        result = jnp.einsum('htk,khd->htd', rounded, value) / total[..., None]
        return jnp.transpose(result, (1, 0, 2)).reshape(block, HEADS * V_DIM).astype(jnp.bfloat16)
    attended = lax.map(one_block, jnp.arange(count, dtype=jnp.int32)).reshape(tokens, HEADS * V_DIM)
    return jnp.dot(attended, out_proj, preferred_element_type=jnp.float32).astype(jnp.bfloat16)
```

```python
import functools

import jax
import jax.numpy as jnp
import numpy as np
from jax import lax
from jax.experimental import pallas as pl
from jax.experimental.pallas import tpu as pltpu
from jax.sharding import PartitionSpec as P

MESH = pl.DeviceIdType.MESH
F32, BF16 = jnp.float32, jnp.bfloat16

ROWS = 128
KV_RANK = 512
NOPE = 128
ROPE = 64
HEADS = 8
Q_RANK = 1536
WINDOW = 9 * ROWS
LAT = KV_RANK + 128
BLOCK = 896
WIDTHS = (512, 384)
OFFS = (0, 512)
SCALE2 = float((NOPE + ROPE) ** (-0.5) * np.log2(np.e))


def tables():
    inverse = 10000.0 ** (-np.arange(32, dtype=np.float64) / 32)
    start = 128.0 * np.arange(32)[:, None] * inverse[None, :]
    step = 1.0 * np.arange(128)[:, None] * inverse[None, :]

    def both(angles):
        return np.concatenate([np.tile(np.cos(angles), 4), np.tile(np.sin(angles), 4)], 1).astype(np.float32)

    return both(start), both(step)


def kernel(
    q_latent, kv_latent, q_gain, kv_gain, q_up, kv_up, out_proj, seg, limit, start_tab, step_tab,
    out,
    ql_v, kvl_v, qg_v, kvg_v, qup_v, kvup_v, seg_v, start_v, step_v,
    lat, bias, query, att, w0, w1, p0, p1, ra0, ra1, rm0, rm1, acc, x0, x1, rx0, rx1,
    load_sem, own_sem, p1_send, p1_recv, ring_send, ring_recv, lat_send, lat_recv,
    att_send, att_recv, ra_send, ra_recv, rm_send, rm_recv, rx_send, rx_recv,
):
    ctx = lax.axis_index("ctx")
    head = lax.axis_index("head")
    z, i = ctx // 4, ctx % 4
    xl, c = i // 2, i % 2
    y, xh = head // 2, head % 2
    wbuf, pbuf, rabuf, rmbuf, xbuf, rxbuf = (w0, w1), (p0, p1), (ra0, ra1), (rm0, rm1), (x0, x1), (rx0, rx1)

    def at_z(step):
        return (((z + step + 8) % 8) * 4 + i, head)

    def at_mate(j):
        return (z * 4 + j, head)

    def at_y(step):
        return (ctx, ((y + step + 4) % 4) * 2 + xh)

    loads = []
    for n, (src, dst) in enumerate(
        ((kv_latent, kvl_v), (kv_gain, kvg_v), (start_tab, start_v), (step_tab, step_v), (seg, seg_v),
         (q_latent, ql_v), (q_gain, qg_v), (q_up, qup_v), (kv_up, kvup_v))
    ):
        copy = pltpu.make_async_copy(src, dst, load_sem.at[n])
        copy.start()
        loads.append(copy)

    def columns(hf, b, mate):
        block = 2 * (mate % 2 + 2 * b) + mate // 2
        return pl.ds(pl.multiple_of(block * BLOCK + OFFS[hf], 128), WIDTHS[hf])

    own_rows = pl.ds(pl.multiple_of(z * 128 + i * 32, 32), 32)

    barrier = pltpu.get_barrier_semaphore()

    def tell(device):
        pl.semaphore_signal(barrier, inc=1, device_id=device, device_id_type=MESH)

    even = (y + c) % 2 == 0
    for step in (-1, -2, 1):
        tell(at_z(step))
    for d in (1, 2, 3):
        tell(at_mate((i + d) % 4))
    for step in (-1, 1):
        tell(at_y(step))
    for other in (0, 1):
        source = 2 * xh + y % 2
        me = (other == xh) & (source == i)

        @pl.when(jnp.logical_not(me))
        def _():
            tell((z * 4 + source, 2 * y + other))

    for n in (0, 1, 2, 3):
        loads[n].wait()
    lane = lax.broadcasted_iota(jnp.int32, (1, 128), 1)
    a = start_v[pl.ds(ctx, 1), :]
    s = step_v[...]
    cos = a[:, :128] * s[:, :128] - a[:, 128:] * s[:, 128:]
    sin = a[:, 128:] * s[:, :128] + a[:, :128] * s[:, 128:]
    low = (lane % 64) < 32
    sin = jnp.where(low, -sin, sin)

    def rotate(v):
        swapped = jnp.where(low, pltpu.roll(v, 96, 1), pltpu.roll(v, 32, 1))
        return v * cos + swapped * sin

    own_lat = pl.ds(pl.multiple_of((8 + i) * 128, 128), 128)
    raw = kvl_v[:, :KV_RANK].astype(F32)
    normed = raw * lax.rsqrt(jnp.mean(raw * raw, axis=-1, keepdims=True) + 1e-06) * kvg_v[...]
    lat[own_lat, :KV_RANK] = normed.astype(BF16)
    kr = kvl_v[:, KV_RANK:].astype(F32)
    lat[own_lat, KV_RANK:] = rotate(jnp.concatenate([kr, kr], axis=1)).astype(BF16)

    pl.semaphore_wait(
        barrier, 8 + jnp.where(even, 4 - (xh == xl).astype(jnp.int32), 0)
    )

    spreads = {}

    def spread(hf, b):
        own = pltpu.make_async_copy(
            out_proj.at[:, columns(hf, b, i)], wbuf[hf].at[b, own_rows, :], own_sem.at[hf, b]
        )
        own.start()
        copies = [own]
        for d in (1, 2, 3):
            mate = (i + d) % 4
            copy = pltpu.make_async_remote_copy(
                src_ref=out_proj.at[:, columns(hf, b, mate)],
                dst_ref=wbuf[hf].at[b, own_rows, :],
                send_sem=p1_send.at[hf, b, d - 1],
                recv_sem=p1_recv.at[hf, b, d - 1],
                device_id=at_mate(mate),
                device_id_type=MESH,
            )
            copy.start()
            copies.append(copy)
        spreads[hf, b] = copies

    def send_latent(n, slot, device):
        rows = pl.ds(pl.multiple_of(slot * 128, 128), 128)
        return lat.at[rows, :], n, device

    def lat_copy(n, src_slot, dst_slot, device):
        src = pl.ds(pl.multiple_of(src_slot * 128, 128), 128)
        dst = pl.ds(pl.multiple_of(dst_slot * 128, 128), 128)
        return pltpu.make_async_remote_copy(
            src_ref=lat.at[src, :], dst_ref=lat.at[dst, :],
            send_sem=lat_send.at[n], recv_sem=lat_recv.at[n],
            device_id=device, device_id_type=MESH,
        )

    ring = {}

    def ring_start(hf, b, way, step):
        shift = -(step - 1) if way == 0 else step - 1
        block = (z + shift + 8) % 8
        rows = pl.ds(pl.multiple_of(block * 128, 128), 128)
        copy = pltpu.make_async_remote_copy(
            src_ref=wbuf[hf].at[b, rows, :], dst_ref=wbuf[hf].at[b, rows, :],
            send_sem=ring_send.at[hf, b, way, step - 1], recv_sem=ring_recv.at[hf, b, way, step - 1],
            device_id=at_z(1 if way == 0 else -1), device_id_type=MESH,
        )
        copy.start()
        ring[hf, b, way, step] = copy

    def ring_event(hf, b, step):
        if step == 1:
            for n, copy in enumerate(spreads[hf, b]):
                if n == 0:
                    copy.wait()
                else:
                    copy.wait_recv()
        for way, last in ((1, 4), (0, 3)):
            if 1 < step <= last + 1:
                ring[hf, b, way, step - 1].wait_recv()
            if step <= last:
                ring_start(hf, b, way, step)

    spread(0, 0)
    one = lat_copy(0, 8 + i, 4 + i, at_z(1))
    two = lat_copy(1, 8 + i, i, at_z(2))
    one.start()
    two.start()
    for d in (1, 2, 3):
        @pl.when(i + d < 4)
        def _():
            lat_copy(1 + d, 8 + i, 8 + i, at_mate(i + d)).start()
    spread(0, 1)

    loads[4].wait()
    everything = seg_v[...]
    starts = []
    for t in range(8):
        below = (everything < t).astype(F32)
        starts.append(jnp.sum(jnp.sum(below, axis=0, keepdims=True), axis=1, keepdims=True).astype(jnp.int32))
    row = lax.broadcasted_iota(jnp.int32, (128, 128), 0)
    column = lax.broadcasted_iota(jnp.int32, (128, 128), 1)
    mine = seg_v[pl.ds(ctx, 1), :]
    qseg = jnp.sum(jnp.where(row == column, mine.astype(F32), 0.0), axis=1, keepdims=True).astype(jnp.int32)
    qplace = ctx * 128 + lax.broadcasted_iota(jnp.int32, (128, 1), 0)
    for n in range(9):
        block = (ctx + 24 + n) % 32
        kseg = seg_v[pl.ds(block, 1), :]
        kplace = block * 128 + lane
        room = jnp.zeros((1, 128), jnp.int32)
        for t in range(8):
            room = room + jnp.where(kseg == t, starts[t] + limit[t], 0)
        kplace_kept = jnp.where(kplace < room, kplace, 1 << 20)
        visible = (qseg == kseg) & (kplace_kept <= qplace)
        bias[:, n * 128:(n + 1) * 128] = jnp.where(visible, 0.0, -1e30)

    ring_event(0, 0, 1)

    one.wait_recv()
    passed = []
    for d in (1, 2, 3):
        copy = lat_copy(4 + d, 4 + i, 4 + i, at_mate((i + d) % 4))
        copy.start()
        passed.append(copy)
    ring_event(0, 1, 1)

    loads[5].wait()
    loads[6].wait()
    raw = ql_v[...].astype(F32)
    qnorm = (raw * lax.rsqrt(jnp.mean(raw * raw, axis=-1, keepdims=True) + 1e-06) * qg_v[...]).astype(BF16)
    two.wait_recv()
    for d in (1, 2, 3):
        @pl.when(i - d >= 0)
        def _():
            lat_copy(7 + d, i, i, at_mate(i - d)).start()
    loads[7].wait()
    half = lane < 64
    for g in range(4):
        three = jnp.dot(qnorm, qup_v[:, g * 384:(g + 1) * 384], preferred_element_type=F32)
        t0, t1, t2 = three[:, :128], three[:, 128:256], three[:, 256:]
        second = jnp.where(half, pltpu.roll(t1, 64, 1), pltpu.roll(t2, 64, 1))
        turned = rotate(jnp.where(half, t1, t2))
        query[2 * g, :, :128] = t0.astype(BF16)
        query[2 * g, :, 128:] = jnp.where(half, turned, 0.0).astype(BF16)
        query[2 * g + 1, :, :128] = second.astype(BF16)
        query[2 * g + 1, :, 128:] = jnp.where(half, 0.0, turned).astype(BF16)

    ring_event(0, 0, 2)
    spread(1, 0)
    ring_event(0, 1, 2)
    spread(1, 1)

    for d in (1, 2, 3):
        @pl.when(i - d >= 0)
        def _():
            lat_copy(1 + d, 8 + i, 8 + i, at_mate(i)).wait_recv()
        passed[d - 1].wait_recv()

        @pl.when(i + d < 4)
        def _():
            lat_copy(7 + d, i, i, at_mate(i)).wait_recv()
    loads[8].wait()
    ring_event(0, 0, 3)

    win = pl.ds(pl.multiple_of(i * 128, 128), WINDOW)
    own_att = pl.ds(pl.multiple_of(i * 128, 128), 128)
    att_copies = []

    def one_head(h):
        keyval = jnp.dot(
            lat[win, :KV_RANK], kvup_v[:, h * 256:(h + 1) * 256], preferred_element_type=F32
        ).astype(BF16)
        keys = jnp.concatenate([keyval[:, :128], lat[win, KV_RANK:]], axis=1)
        scores = lax.dot_general(query[h], keys, (((1,), (1,)), ((), ())), preferred_element_type=F32)
        masked = scores * SCALE2 + bias[...]
        weights = jnp.exp2(masked - jnp.max(masked, axis=1, keepdims=True))
        total = jnp.sum(weights, axis=1, keepdims=True)
        summed = jnp.dot(weights.astype(BF16), keyval[:, 128:], preferred_element_type=F32)
        att[own_att, h * 128:(h + 1) * 128] = (summed / total).astype(BF16)

    events = {1: (0, 1, 3), 2: (0, 0, 4), 3: (1, 0, 1), 4: (0, 1, 4), 5: (1, 1, 1), 7: (1, 0, 2)}
    for h in range(8):
        one_head(h)
        if h % 2 == 1:
            g = h // 2
            for d in (1, 2, 3):
                part = att.at[own_att, g * 256:(g + 1) * 256]
                copy = pltpu.make_async_remote_copy(
                    src_ref=part, dst_ref=part, send_sem=att_send.at[g, d - 1], recv_sem=att_recv.at[g, d - 1],
                    device_id=at_mate((i + d) % 4), device_id_type=MESH,
                )
                copy.start()
                att_copies.append(copy)
        if h in events:
            ring_event(*events[h])

    def partial(hf, b):
        return jnp.dot(att[...], wbuf[hf][b], preferred_element_type=F32)

    def ra_copy(hf, side):
        return pltpu.make_async_remote_copy(
            src_ref=pbuf[hf].at[0, side * 256:(side + 1) * 256, :], dst_ref=rabuf[hf].at[side],
            send_sem=ra_send.at[hf, side], recv_sem=ra_recv.at[hf, side],
            device_id=at_y(1 - 2 * side), device_id_type=MESH,
        )

    def rm_copy(hf, side):
        return pltpu.make_async_remote_copy(
            src_ref=pbuf[hf].at[side], dst_ref=rmbuf[hf].at[side],
            send_sem=rm_send.at[hf, side], recv_sem=rm_recv.at[hf, side],
            device_id=at_y(1 - 2 * side), device_id_type=MESH,
        )

    def rx_pieces(hf, j):
        src = xbuf[hf].at[j * 128:(j + 1) * 128, :]
        dst = rxbuf[hf].at[xh]
        self_copy = pltpu.make_async_copy(src, dst, rx_recv.at[hf, xh])
        far_copy = pltpu.make_async_remote_copy(
            src_ref=src, dst_ref=dst, send_sem=rx_send.at[hf, j], recv_sem=rx_recv.at[hf, xh],
            device_id=(z * 4 + j, 2 * y + xl), device_id_type=MESH,
        )
        return self_copy, far_copy, (xh == xl) & (i == j)

    def reduce_first(hf):
        w = WIDTHS[hf]
        toward_next = ((y + 1 - c + 4) % 4) // 2
        own = ((y - c + 4) % 4) // 2

        @pl.when(even)
        def _():
            pbuf[hf][0] = partial(hf, 1 - own).astype(BF16)
            ra_copy(hf, 0).start()
            ra_copy(hf, 1).start()
            acc[:, :w] = partial(hf, own)

        @pl.when(jnp.logical_not(even))
        def _():
            for side, b in ((0, toward_next), (1, 1 - toward_next)):
                acc[:, :w] = partial(hf, b)
                ra_copy(hf, side).wait_recv()
                here = slice(side * 256, (side + 1) * 256)
                there = slice((1 - side) * 256, (2 - side) * 256)
                pbuf[hf][side, here, :] = (acc[here, :w] + rabuf[hf][side].astype(F32)).astype(BF16)
                pbuf[hf][side, there, :] = acc[there, :w].astype(BF16)
                rm_copy(hf, side).start()

    def reduce_second(hf):
        w = WIDTHS[hf]

        @pl.when(even)
        def _():
            rm_copy(hf, 0).wait_recv()
            rm_copy(hf, 1).wait_recv()
            xbuf[hf][...] = (
                acc[:, :w] + rmbuf[hf][0].astype(F32) + rmbuf[hf][1].astype(F32)
            ).astype(BF16)
            for j in range(4):
                self_copy, far_copy, me = rx_pieces(hf, j)

                @pl.when(me)
                def _():
                    self_copy.start()

                @pl.when(jnp.logical_not(me))
                def _():
                    far_copy.start()

    def reduce_last(hf):
        w = WIDTHS[hf]
        for n in range(2):
            pltpu.make_async_copy(rxbuf[hf].at[n], rxbuf[hf].at[n], rx_recv.at[hf, n]).wait()
        out[:, OFFS[hf]:OFFS[hf] + w] = (rxbuf[hf][0].astype(F32) + rxbuf[hf][1].astype(F32)).astype(BF16)

    for copy in att_copies:
        copy.wait_recv()
    ring_event(0, 0, 5)
    ring_event(1, 1, 2)
    ring_event(0, 1, 5)
    reduce_first(0)
    ring_event(1, 0, 3)
    ring_event(1, 1, 3)
    reduce_second(0)
    ring_event(1, 0, 4)
    ring_event(1, 1, 4)
    reduce_last(0)
    ring_event(1, 0, 5)
    ring_event(1, 1, 5)
    reduce_first(1)
    reduce_second(1)
    reduce_last(1)

    for copies in spreads.values():
        for copy in copies[1:]:
            copy.wait_send()
    for copy in ring.values():
        copy.wait_send()
    for copy in (one, two, *passed, *att_copies):
        copy.wait_send()
    for d in (1, 2, 3):
        @pl.when(i + d < 4)
        def _():
            lat_copy(1 + d, 8 + i, 8 + i, at_mate(i)).wait_send()

        @pl.when(i - d >= 0)
        def _():
            lat_copy(7 + d, i, i, at_mate(i)).wait_send()

    @pl.when(even)
    def _():
        for hf in (0, 1):
            ra_copy(hf, 0).wait_send()
            ra_copy(hf, 1).wait_send()
            for j in range(4):
                _, far_copy, me = rx_pieces(hf, j)

                @pl.when(jnp.logical_not(me))
                def _():
                    far_copy.wait_send()

    @pl.when(jnp.logical_not(even))
    def _():
        for hf in (0, 1):
            rm_copy(hf, 0).wait_send()
            rm_copy(hf, 1).wait_send()


def body(q_latent, kv_latent, q_gain, kv_gain, q_up, kv_up, out_proj, segment_ids, trace_limit):
    start_tab, step_tab = tables()
    any_spec = pl.BlockSpec(memory_space=pl.ANY)
    dma = pltpu.SemaphoreType.DMA
    wa, wb = WIDTHS
    scratch = [
        pltpu.VMEM((ROWS, Q_RANK), BF16),
        pltpu.VMEM((ROWS, KV_RANK + ROPE), BF16),
        pltpu.VMEM((1, Q_RANK), F32),
        pltpu.VMEM((1, KV_RANK), F32),
        pltpu.VMEM((Q_RANK, HEADS * (NOPE + ROPE)), BF16),
        pltpu.VMEM((KV_RANK, HEADS * 256), BF16),
        pltpu.VMEM((32, 128), jnp.int32),
        pltpu.VMEM((32, 256), F32),
        pltpu.VMEM((128, 256), F32),
        pltpu.VMEM((12 * ROWS, LAT), BF16),
        pltpu.VMEM((ROWS, WINDOW), F32),
        pltpu.VMEM((HEADS, ROWS, 256), BF16),
        pltpu.VMEM((4 * ROWS, HEADS * 128), BF16),
        pltpu.VMEM((2, 1024, wa), BF16),
        pltpu.VMEM((2, 1024, wb), BF16),
        pltpu.VMEM((2, 512, wa), BF16),
        pltpu.VMEM((2, 512, wb), BF16),
        pltpu.VMEM((2, 256, wa), BF16),
        pltpu.VMEM((2, 256, wb), BF16),
        pltpu.VMEM((2, 512, wa), BF16),
        pltpu.VMEM((2, 512, wb), BF16),
        pltpu.VMEM((512, wa), F32),
        pltpu.VMEM((512, wa), BF16),
        pltpu.VMEM((512, wb), BF16),
        pltpu.VMEM((2, ROWS, wa), BF16),
        pltpu.VMEM((2, ROWS, wb), BF16),
        dma((9,)),
        dma((2, 2)),
        dma((2, 2, 3)),
        dma((2, 2, 3)),
        dma((2, 2, 2, 4)),
        dma((2, 2, 2, 4)),
        dma((11,)),
        dma((11,)),
        dma((4, 3)),
        dma((4, 3)),
        dma((2, 2)),
        dma((2, 2)),
        dma((2, 2)),
        dma((2, 2)),
        dma((2, 4)),
        dma((2, 2)),
    ]
    return pl.pallas_call(
        kernel,
        out_shape=jax.ShapeDtypeStruct((ROWS, BLOCK), BF16),
        in_specs=[any_spec] * 8 + [pl.BlockSpec(memory_space=pltpu.SMEM)] + [any_spec] * 2,
        out_specs=pl.BlockSpec(memory_space=pltpu.VMEM),
        scratch_shapes=scratch,
        compiler_params=pltpu.CompilerParams(
            collective_id=0, has_side_effects=True, vmem_limit_bytes=56 * 2**20
        ),
        name="latent_attention",
    )(
        q_latent, kv_latent, q_gain.reshape(1, Q_RANK), kv_gain.reshape(1, KV_RANK), q_up, kv_up, out_proj,
        segment_ids.reshape(32, 128), trace_limit, jnp.asarray(start_tab), jnp.asarray(step_tab),
    )


def solution(mesh):
    in_specs = (
        P("ctx", None),
        P("ctx", None),
        P(),
        P(),
        P(None, "head"),
        P(None, "head"),
        P(("head", "ctx"), None),
        P(),
        P(),
    )
    return jax.shard_map(body, mesh=mesh, in_specs=in_specs, out_specs=P("ctx", "head"), check_vma=False)
```

```python
import functools

import jax
import jax.numpy as jnp
import numpy as np
from jax import lax
from jax.experimental import pallas as pl
from jax.experimental.pallas import tpu as pltpu
from jax.sharding import PartitionSpec as P

MESH = pl.DeviceIdType.MESH
F32, BF16 = jnp.float32, jnp.bfloat16

ROWS = 128
KV_RANK = 512
NOPE = 128
ROPE = 64
HEADS = 8
Q_RANK = 1536
WINDOW = 9 * ROWS
LAT = KV_RANK + 128
BLOCK = 896
WIDTHS = (128, 256, 256, 128, 128)
OFFS = (0, 128, 384, 640, 768)
PARTS = len(WIDTHS)
SCALE2 = float((NOPE + ROPE) ** (-0.5) * np.log2(np.e))


def tables():
    inverse = 10000.0 ** (-np.arange(32, dtype=np.float64) / 32)
    start = 128.0 * np.arange(32)[:, None] * inverse[None, :]
    step = 1.0 * np.arange(128)[:, None] * inverse[None, :]

    def both(angles):
        return np.concatenate([np.tile(np.cos(angles), 4), np.tile(np.sin(angles), 4)], 1).astype(np.float32)

    return both(start), both(step)


def kernel(
    q_latent, kv_latent, q_gain, kv_gain, q_up, kv_up, out_proj, seg, limit, start_tab, step_tab,
    out,
    ql_v, kvl_v, qg_v, kvg_v, qup_v, kvup_v, seg_v, start_v, step_v, lat, keyval, bias, query, att, final,
    wbuf, pbuf, rabuf, rmbuf, acc,
    load_sem, own_sem, spread_send, spread_recv, ring_send, ring_recv, lat_send, lat_recv,
    att_send, att_recv, ra_send, ra_recv, rm_send, rm_recv, rx_send, rx_recv,
):
    ctx = lax.axis_index("ctx")
    head = lax.axis_index("head")
    z, i = ctx // 4, ctx % 4
    xl, c = i // 2, i % 2
    y, xh = head // 2, head % 2
    x = 2 * xh + xl

    def at_z(step):
        return (((z + step + 8) % 8) * 4 + i, head)

    def at_x(there, core):
        return (z * 4 + (there % 2) * 2 + core, y * 2 + there // 2)

    def at_y(step):
        return (ctx, ((y + step + 4) % 4) * 2 + xh)

    sent = []

    def send(src, dst, send_sem, recv_sem, device):
        copy = pltpu.make_async_remote_copy(
            src_ref=src, dst_ref=dst, send_sem=send_sem, recv_sem=recv_sem, device_id=device, device_id_type=MESH
        )
        copy.start()
        sent.append(copy)
        return copy

    loads = []
    for n, (src, dst) in enumerate(
        ((kv_latent, kvl_v), (kv_gain, kvg_v), (start_tab, start_v), (step_tab, step_v), (seg, seg_v),
         (q_latent, ql_v), (q_gain, qg_v), (q_up, qup_v), (kv_up, kvup_v))
    ):
        copy = pltpu.make_async_copy(src, dst, load_sem.at[n])
        copy.start()
        loads.append(copy)

    barrier = pltpu.get_barrier_semaphore()

    def tell(device):
        pl.semaphore_signal(barrier, inc=1, device_id=device, device_id_type=MESH)

    for step in (-1, 1):
        tell(at_z(step))
        tell(at_y(step))
    place = x * 2 + c
    for d in range(1, 8):
        other = (place + d) % 8
        tell(at_x(other // 2, other % 2))

    for n in (0, 1, 2, 3):
        loads[n].wait()
    lane = lax.broadcasted_iota(jnp.int32, (1, 128), 1)
    a = start_v[pl.ds(ctx, 1), :]
    s = step_v[...]
    cos = a[:, :128] * s[:, :128] - a[:, 128:] * s[:, 128:]
    sin = a[:, 128:] * s[:, :128] + a[:, :128] * s[:, 128:]
    low = (lane % 64) < 32
    sin = jnp.where(low, -sin, sin)

    def rotate(v):
        swapped = jnp.where(low, pltpu.roll(v, 96, 1), pltpu.roll(v, 32, 1))
        return v * cos + swapped * sin

    def slot(p, j):
        return pl.ds(pl.multiple_of((p * 4 + j) * 128, 128), 128)

    raw = jnp.transpose(kvl_v[:KV_RANK, :].astype(F32))
    normed = raw * lax.rsqrt(jnp.mean(raw * raw, axis=-1, keepdims=True) + 1e-06) * kvg_v[...]
    lat[slot(2, i), :KV_RANK] = normed.astype(BF16)
    kr = kvl_v[KV_RANK:, :].astype(F32)
    lat[slot(2, i), KV_RANK:] = rotate(jnp.transpose(jnp.concatenate([kr, kr], axis=0))).astype(BF16)

    pl.semaphore_wait(barrier, 11)

    def lat_z(p):
        part_src, part_dst = lat.at[slot(p, i), :], lat.at[slot(p - 1, i), :]
        return send(part_src, part_dst, lat_send.at[p - 1, 0], lat_recv.at[p - 1, 0], at_z(1))

    def lat_spread(p):
        start = (p * 4 + i) * 128
        copies = []
        for n in (0, 1):
            part = lat.at[pl.ds(pl.multiple_of(start + n * 64, 64), 64), :]
            copies.append(
                send(part, part, lat_send.at[p, 1 + n], lat_recv.at[p, 1 + n], at_x((x + 1 + 2 * n) % 4, c))
            )
        part = lat.at[slot(p, i), :]
        copies.append(send(part, part, lat_send.at[p, 3], lat_recv.at[p, 3], at_x(x, 1 - c)))
        return copies

    def lat_pass(p, copies):
        copies[0].wait_recv()
        copies[1].wait_recv()
        part = lat.at[slot(p, 2 * (1 - xl) + c), :]
        copies.append(send(part, part, lat_send.at[p, 4], lat_recv.at[p, 4], at_x(x, 1 - c)))

    own_rows = pl.ds(pl.multiple_of(i * 32, 32), 32)
    spreads = {}

    def columns(k, there, core):
        block = 2 * (there % 2 + 2 * core) + there // 2
        return pl.ds(pl.multiple_of(block * BLOCK + OFFS[k], 128), WIDTHS[k])

    def spread(k):
        dst = wbuf[k].at[z, xh, own_rows, :]
        own = pltpu.make_async_copy(out_proj.at[:, columns(k, x, c)], dst, own_sem.at[k])
        own.start()
        copies = []
        for d in range(1, 8):
            other = (place + d) % 8
            there, core = other // 2, other % 2
            copies.append(
                send(out_proj.at[:, columns(k, there, core)], dst, spread_send.at[k, d - 1],
                     spread_recv.at[k, d - 1], at_x(there, core))
            )
        spreads[k] = (own, copies)

    ring = {}

    def ring_event(k, step, way):
        if step == 1 and way == 1:
            own, copies = spreads[k]
            own.wait()
            for copy in copies:
                copy.wait_recv()
        if step > 1:
            ring[k, way, step - 1].wait_recv()
        if step <= 3 + way:
            block = (z + (step - 1) * (2 * way - 1) + 8) % 8
            part = wbuf[k].at[block]
            ring[k, way, step] = send(
                part, part, ring_send.at[k, way, step - 1], ring_recv.at[k, way, step - 1], at_z(1 - 2 * way)
            )

    def plus(*events):
        for k, step in events:
            ring_event(k, step, 0)

    def minus(*events):
        for k, step in events:
            ring_event(k, step, 1)

    spread(0)
    lat_z(2)
    lat2 = lat_spread(2)
    spread(1)
    spread(2)
    spread(3)
    spread(4)

    loads[4].wait()
    everything = seg_v[...]
    starts = []
    for t in range(8):
        below = (everything < t).astype(F32)
        starts.append(jnp.sum(jnp.sum(below, axis=0, keepdims=True), axis=1, keepdims=True).astype(jnp.int32))
    row = lax.broadcasted_iota(jnp.int32, (128, 128), 0)
    column = lax.broadcasted_iota(jnp.int32, (128, 128), 1)
    mine = seg_v[pl.ds(ctx, 1), :]
    qseg = jnp.sum(jnp.where(row == column, mine.astype(F32), 0.0), axis=1, keepdims=True).astype(jnp.int32)
    qplace = ctx * 128 + lax.broadcasted_iota(jnp.int32, (128, 1), 0)
    for n in range(9):
        block = (ctx + 24 + n) % 32
        kseg = seg_v[pl.ds(block, 1), :]
        kplace = block * 128 + lane
        room = jnp.zeros((1, 128), jnp.int32)
        for t in range(8):
            room = room + jnp.where(kseg == t, starts[t] + limit[t], 0)
        kplace_kept = jnp.where(kplace < room, kplace, 1 << 20)
        visible = (qseg == kseg) & (kplace_kept <= qplace)
        bias[:, n * 128:(n + 1) * 128] = jnp.where(visible, 0.0, -1e30)

    minus((0, 1), (1, 1))
    lat_pass(2, lat2)
    lat_first = pltpu.make_async_remote_copy(
        src_ref=lat.at[slot(1, i), :], dst_ref=lat.at[slot(1, i), :], send_sem=lat_send.at[1, 0],
        recv_sem=lat_recv.at[1, 0], device_id=at_z(1), device_id_type=MESH,
    )
    lat_first.wait_recv()
    lat_second = lat_z(1)
    lat1 = lat_spread(1)
    minus((2, 1), (0, 2), (3, 1), (4, 1))

    loads[5].wait()
    loads[6].wait()
    raw = ql_v[...].astype(F32)
    q_gain_row = jnp.concatenate([qg_v[t:t + 1, :] for t in range(Q_RANK // 128)], axis=1)
    qnorm = (raw * lax.rsqrt(jnp.mean(raw * raw, axis=-1, keepdims=True) + 1e-06) * q_gain_row).astype(BF16)
    loads[7].wait()
    half = lane < 64

    def queries(g):
        three = jnp.dot(qnorm, qup_v[:, g * 384:(g + 1) * 384], preferred_element_type=F32)
        t0, t1, t2 = three[:, :128], three[:, 128:256], three[:, 256:]
        second = jnp.where(half, pltpu.roll(t1, 64, 1), pltpu.roll(t2, 64, 1))
        turned = rotate(jnp.where(half, t1, t2))
        query[2 * g, :, :128] = t0.astype(BF16)
        query[2 * g, :, 128:] = jnp.where(half, turned, 0.0).astype(BF16)
        query[2 * g + 1, :, :128] = second.astype(BF16)
        query[2 * g + 1, :, 128:] = jnp.where(half, 0.0, turned).astype(BF16)

    def project(p):
        for n in range(4):
            cols = slice(n * 512, (n + 1) * 512)
            keyval[p * 512:(p + 1) * 512, cols] = jnp.dot(
                lat[p * 512:(p + 1) * 512, :KV_RANK], kvup_v[:, cols], preferred_element_type=F32
            ).astype(BF16)

    for g in range(4):
        queries(g)
    minus((1, 2))
    lat_pass(1, lat1)
    loads[8].wait()
    lat2[2].wait_recv()
    lat2[3].wait_recv()
    project(2)
    lat_second.wait_recv()
    lat0 = lat_spread(0)
    plus((0, 1), (1, 1), (2, 1), (3, 1), (4, 1))
    minus((2, 2))
    lat1[2].wait_recv()
    lat1[3].wait_recv()
    project(1)
    lat_pass(0, lat0)
    minus((3, 2), (4, 2))
    plus((0, 2))
    lat0[2].wait_recv()
    lat0[3].wait_recv()
    project(0)

    win = pl.ds(pl.multiple_of(i * 128, 128), WINDOW)

    def one_head(h):
        keys = jnp.concatenate([keyval[win, h * 256:h * 256 + 128], lat[win, KV_RANK:]], axis=1)
        scores = lax.dot_general(query[h], keys, (((1,), (1,)), ((), ())), preferred_element_type=F32)
        masked = scores * SCALE2 + bias[...]
        weights = jnp.exp2(masked - jnp.max(masked, axis=1, keepdims=True))
        total = jnp.sum(weights, axis=1, keepdims=True)
        summed = jnp.dot(weights.astype(BF16), keyval[win, h * 256 + 128:(h + 1) * 256], preferred_element_type=F32)
        rows = pl.ds(pl.multiple_of(i * 128, 128), 128)
        att[xh, rows, h * 128:(h + 1) * 128] = (summed / total).astype(BF16)

    def att_part(g, there, first=0, count=128):
        begin = ((there % 2) * 2 + c) * 128 + first
        return att.at[there // 2, pl.ds(pl.multiple_of(begin, 64), count), g * 256:(g + 1) * 256]

    att1, att2 = {}, {}

    def att_send_own(g):
        part = att_part(g, x)
        att1[g] = [
            send(part, part, att_send.at[g, n], att_recv.at[g, n], at_x((x + 1 + n) % 4, c)) for n in range(3)
        ]
        att2[g] = [send(part, part, att_send.at[g, 3], att_recv.at[g, 3], at_x(x, 1 - c))]

    def att_pass(g):
        for n in (0, 2, 1):
            att1[g][n].wait_recv()
            part = att_part(g, (x + 3 - n) % 4)
            att2[g].append(send(part, part, att_send.at[g, 4 + n], att_recv.at[g, 4 + n], at_x(x, 1 - c)))

    one_head(0)
    plus((1, 2))
    one_head(1)
    att_send_own(0)
    minus((0, 3))
    plus((2, 2))
    one_head(2)
    minus((1, 3))
    one_head(3)
    att_send_own(1)
    plus((3, 2), (4, 2))
    minus((2, 3))
    one_head(4)
    att_pass(0)
    minus((3, 3))
    one_head(5)
    att_send_own(2)
    plus((0, 3))
    minus((4, 3))
    one_head(6)
    att_pass(1)
    plus((1, 3))
    one_head(7)
    att_send_own(3)
    minus((0, 4))
    plus((2, 3))

    target = xl + 2 * c
    role = (y - target + 4) % 4

    def ra_copy(k, side):
        return pltpu.make_async_remote_copy(
            src_ref=pbuf[k].at[side * 256:(side + 1) * 256, :], dst_ref=rabuf[k],
            send_sem=ra_send.at[k, side], recv_sem=ra_recv.at[k],
            device_id=at_y(1 - 2 * side), device_id_type=MESH,
        )

    def rm_copy(k, side):
        return pltpu.make_async_remote_copy(
            src_ref=pbuf[k], dst_ref=rmbuf[k].at[side],
            send_sem=rm_send.at[k, side], recv_sem=rm_recv.at[k, side],
            device_id=at_y(1 - 2 * side), device_id_type=MESH,
        )

    def rx_copy(k, d):
        j = (i + d) % 4
        return pltpu.make_async_remote_copy(
            src_ref=pbuf[k].at[pl.ds(pl.multiple_of(j * 128, 128), 128), :],
            dst_ref=final.at[:, OFFS[k]:OFFS[k] + WIDTHS[k]],
            send_sem=rx_send.at[k, d - 1], recv_sem=rx_recv.at[k],
            device_id=(z * 4 + j, head), device_id_type=MESH,
        )

    def reduce_first(k):
        w = wbuf[k]
        acc[k][...] = jnp.dot(
            att[0], w[:, 0].reshape(1024, WIDTHS[k]), preferred_element_type=F32
        ) + jnp.dot(att[1], w[:, 1].reshape(1024, WIDTHS[k]), preferred_element_type=F32)

        @pl.when(role == 2)
        def _():
            pbuf[k][...] = acc[k][...].astype(BF16)
            ra_copy(k, 0).start()
            ra_copy(k, 1).start()

    def reduce_second(k):
        for mine, side in ((3, 0), (1, 1)):
            @pl.when(role == mine)
            def _():
                here = slice(side * 256, (side + 1) * 256)
                there = slice((1 - side) * 256, (2 - side) * 256)
                pbuf[k][there, :] = acc[k][there, :].astype(BF16)
                ra_copy(k, side).wait_recv()
                pbuf[k][here, :] = (acc[k][here, :] + rabuf[k][...].astype(F32)).astype(BF16)
                rm_copy(k, side).start()

    def reduce_third(k):
        @pl.when(role == 0)
        def _():
            rm_copy(k, 0).wait_recv()
            rm_copy(k, 1).wait_recv()
            pbuf[k][...] = (acc[k][...] + rmbuf[k][0].astype(F32) + rmbuf[k][1].astype(F32)).astype(BF16)
            for d in (1, 2, 3):
                rx_copy(k, d).start()

    def reduce_last(k):
        cols = slice(OFFS[k], OFFS[k] + WIDTHS[k])

        @pl.when(role == 0)
        def _():
            out[:, cols] = pbuf[k][pl.ds(pl.multiple_of(i * 128, 128), 128), :]

        @pl.when(role != 0)
        def _():
            rx_copy(k, 1).wait_recv()
            out[:, cols] = final[:, cols]

    att_pass(2)
    minus((1, 4))
    plus((3, 3), (4, 3))
    att_pass(3)
    minus((2, 4))
    for g in range(4):
        for copy in att2[g]:
            copy.wait_recv()
    minus((3, 4), (4, 4))
    plus((0, 4))
    minus((0, 5))
    reduce_first(0)
    plus((1, 4))
    minus((1, 5))
    reduce_first(1)
    reduce_second(0)
    plus((2, 4))
    minus((2, 5))
    reduce_first(2)
    reduce_second(1)
    reduce_third(0)
    plus((3, 4))
    minus((3, 5))
    reduce_first(3)
    reduce_second(2)
    reduce_third(1)
    plus((4, 4))
    minus((4, 5))
    reduce_first(4)
    reduce_second(3)
    reduce_third(2)
    reduce_second(4)
    reduce_third(3)
    reduce_third(4)
    for k in range(PARTS):
        reduce_last(k)

    for copy in sent:
        copy.wait_send()

    @pl.when(role == 2)
    def _():
        for k in range(PARTS):
            ra_copy(k, 0).wait_send()
            ra_copy(k, 1).wait_send()

    for mine, side in ((3, 0), (1, 1)):
        @pl.when(role == mine)
        def _():
            for k in range(PARTS):
                rm_copy(k, side).wait_send()

    @pl.when(role == 0)
    def _():
        for k in range(PARTS):
            for d in (1, 2, 3):
                rx_copy(k, d).wait_send()


def body(q_latent, kv_latent, q_gain, kv_gain, q_up, kv_up, out_proj, segment_ids, trace_limit):
    start_tab, step_tab = tables()
    any_spec = pl.BlockSpec(memory_space=pl.ANY)
    dma = pltpu.SemaphoreType.DMA
    scratch = [
        pltpu.VMEM((ROWS, Q_RANK), BF16),
        pltpu.VMEM((KV_RANK + ROPE, ROWS), BF16),
        pltpu.VMEM((Q_RANK // 128, 128), F32),
        pltpu.VMEM((1, KV_RANK), F32),
        pltpu.VMEM((Q_RANK, HEADS * (NOPE + ROPE)), BF16),
        pltpu.VMEM((KV_RANK, HEADS * 256), BF16),
        pltpu.VMEM((32, 128), jnp.int32),
        pltpu.VMEM((32, 256), F32),
        pltpu.VMEM((128, 256), F32),
        pltpu.VMEM((12 * ROWS, LAT), BF16),
        pltpu.VMEM((12 * ROWS, HEADS * 256), BF16),
        pltpu.VMEM((ROWS, WINDOW), F32),
        pltpu.VMEM((HEADS, ROWS, 256), BF16),
        pltpu.VMEM((2, 4 * ROWS, HEADS * 128), BF16),
        pltpu.VMEM((ROWS, BLOCK), BF16),
        [pltpu.VMEM((8, 2, 128, w), BF16) for w in WIDTHS],
        [pltpu.VMEM((512, w), BF16) for w in WIDTHS],
        [pltpu.VMEM((256, w), BF16) for w in WIDTHS],
        [pltpu.VMEM((2, 512, w), BF16) for w in WIDTHS],
        [pltpu.VMEM((512, w), F32) for w in WIDTHS],
        dma((9,)),
        dma((PARTS,)),
        dma((PARTS, 7)),
        dma((PARTS, 7)),
        dma((PARTS, 2, 4)),
        dma((PARTS, 2, 4)),
        dma((3, 5)),
        dma((3, 5)),
        dma((4, 8)),
        dma((4, 8)),
        dma((PARTS, 2)),
        dma((PARTS,)),
        dma((PARTS, 2)),
        dma((PARTS, 2)),
        dma((PARTS, 3)),
        dma((PARTS,)),
    ]
    return pl.pallas_call(
        kernel,
        out_shape=jax.ShapeDtypeStruct((ROWS, BLOCK), BF16),
        in_specs=[any_spec] * 8 + [pl.BlockSpec(memory_space=pltpu.SMEM)] + [any_spec] * 2,
        out_specs=pl.BlockSpec(memory_space=pltpu.VMEM),
        scratch_shapes=scratch,
        compiler_params=pltpu.CompilerParams(
            collective_id=0, has_side_effects=True, vmem_limit_bytes=56 * 2**20
        ),
        name="latent_attention",
    )(
        q_latent, kv_latent.T, q_gain.reshape(Q_RANK // 128, 128), kv_gain.reshape(1, KV_RANK), q_up, kv_up,
        out_proj, segment_ids.reshape(32, 128), trace_limit, jnp.asarray(start_tab), jnp.asarray(step_tab),
    )


def solution(mesh):
    in_specs = (
        P("ctx", None),
        P("ctx", None),
        P(),
        P(),
        P(None, "head"),
        P(None, "head"),
        P(("head", "ctx"), None),
        P(),
        P(),
    )
    return jax.shard_map(body, mesh=mesh, in_specs=in_specs, out_specs=P("ctx", "head"), check_vma=False)
```
